32 devices in a mesh: space: 8 (over z, x), chan: 4 (over y, core).
Axes of the slice: x: 2, y: 2, z: 4, core: 2. Of those that a mesh axis runs over, the one named last changes fastest.
Arguments:
- features: bfloat16 [1024, 512], P('space', 'chan'), may hold values from -6 to 6
- mask: int32 [1024], P('space'), may hold values 0 or 1
- rulebook: int32 [16, 27], P('space'), may hold values from -1 to 15, as said below
- weight_first: bfloat16 [512, 27, 512], P('space', None, 'chan'), may hold values from -0.0546875 to 0.0546875
- weight_second: bfloat16 [512, 27, 512], P('space', None, 'chan'), may hold values from -0.0546875 to 0.0546875
- cotangent: bfloat16 [1024, 512], P('space', 'chan'), may hold values from -6 to 6
Outputs:
- output: bfloat16 [1024, 512], P('space', 'chan')
- features_grad: bfloat16 [1024, 512], P('space', 'chan')
- weight_first_grad: float32 [512, 27, 512], P('space', None, 'chan')
- weight_second_grad: float32 [512, 27, 512], P('space', None, 'chan')
The draws below stay inside these ranges and needn't reach their ends.
Inputs may be any that keep to these rules, and one draw needn't show every extreme that they name: `rulebook`: entry [b, c] is the brick that feeds brick b through brick offset c, or -1 for none; entry 13 is b itself. A brick of another device belongs to a device s one or two indices away; if it feeds the device s + 1, s + 2, s - 1 or s - 2 (k = 0, 1, 2, 3 respectively), it is brick s * 2 + ((k + h) mod 2) for some h below 1.
All inputs are finite; a program needn't handle non-finite values. No bound on the sum of `mask` on one device may be relied on, other than what follows from the above.
Results may differ from the reference program's by a relative error of at most 0.005.
Values may be sent and summed in bfloat16 or wider, within the bound.
A program may use at most 128 MiB of HBM per device.

```python
import jax
import jax.numpy as jnp
import numpy as np
from jax import lax

C = 512
OFFSETS = 27
BR_DEV = 2
HB = 1
BRICKS = 16
VOXELS = 1024
N_SPACE = 8


def draw_rulebook(key, part):
    base = jax.random.fold_in(key, 23)
    kinds = jax.random.randint(jax.random.fold_in(base, 1), (BRICKS, 27), 0, 10)
    slots = jax.random.randint(jax.random.fold_in(base, 2), (BRICKS, 27), 0, HB)
    locals_drawn = jax.random.randint(jax.random.fold_in(base, 3), (BRICKS, 27), 0, BR_DEV)
    device = (jnp.arange(BRICKS, dtype=jnp.int32) // BR_DEV)[:, None]
    steps = jnp.array([1, 2, -1, -2], jnp.int32)
    position = (kinds - 3) % 4
    source = device - steps[position]
    valid = (source >= 0) & (source < N_SPACE)
    clipped = jnp.clip(source, 0, N_SPACE - 1)
    remote = clipped * BR_DEV + (position * HB + slots) % BR_DEV
    local_brick = device * BR_DEV + locals_drawn
    is_remote = (kinds >= 3) & (kinds < 9) & valid
    chosen = jnp.where(kinds == 9, -1, jnp.where(is_remote, remote, local_brick))
    center = (jnp.arange(27) == 13)[None, :]
    itself = jnp.arange(BRICKS, dtype=jnp.int32)[:, None]
    return jnp.where(center, itself, chosen).astype(jnp.int32)


def touch_ends(result, stream_key, least, top_value):
    dims = result.shape
    spot = [jax.random.randint(jax.random.fold_in(stream_key, axis), (), 0, dims[axis]) for axis in range(len(dims))]
    result = result.at[tuple(spot)].set(least)
    longest = dims.index(max(dims))
    spot[longest] = (spot[longest] + 1) % dims[longest]
    return result.at[tuple(spot)].set(top_value)


def block_levels(stream_key, extent, split, smallest, top_value):
    loudness = 1.0
    for dim, parts in split:
        draws = jax.random.uniform(jax.random.fold_in(jax.random.fold_in(stream_key, 6), dim), (parts,), jnp.float32, smallest / len(split), top_value / len(split))
        loudness = loudness * jnp.repeat(jnp.exp(draws), extent[dim] // parts).reshape((-1,) + (1,) * (len(extent) - 1 - dim))
    return loudness


def scatter_about(stream_key, extent, scale, most, shards=(), kind=jnp.bfloat16):
    result = jax.random.normal(stream_key, extent, jnp.float32) * scale
    if len(shards) > 0:
        result = block_levels(stream_key, extent, shards, -0.22, 0.18) * result
    return jnp.clip(result, min=-most, max=most).astype(kind)


def setup_inputs(seed: int = 0) -> dict:
    key_list = jax.random.split(jax.random.key(seed), 7)
    features = scatter_about(key_list[0], (VOXELS, C), 1.0, 6.0, ((0, 8), (1, 4)))
    mask = touch_ends((jax.random.randint(key_list[1], (VOXELS,), 0, 4) < 3).astype(jnp.int32), jax.random.fold_in(key_list[1], 1), 0, 1)
    rulebook = draw_rulebook(jax.random.fold_in(key_list[6], 71), 0)
    weight_first = scatter_about(key_list[3], (C, OFFSETS, C), (OFFSETS * C) ** -0.5, 0.0546875, ((0, 8), (2, 4)))
    weight_second = scatter_about(key_list[4], (C, OFFSETS, C), (OFFSETS * C) ** -0.5, 0.0546875, ((0, 8), (2, 4)))
    cotangent = scatter_about(key_list[5], (VOXELS, C), 1.0, 6.0, ((0, 8), (1, 4)))
    return dict(features=features, mask=mask, rulebook=rulebook, weight_first=weight_first, weight_second=weight_second, cotangent=cotangent)


def offset_tables():
    brick_table = np.zeros((27, 64), np.int32)
    cell_table = np.zeros((27, 64), np.int32)
    for offset in range(27):
        moves = (offset // 9 - 1, offset // 3 % 3 - 1, offset % 3 - 1)
        for voxel in range(64):
            cells = (voxel // 16, voxel // 4 % 4, voxel % 4)
            target = [cells[axis_number] + moves[axis_number] for axis_number in range(3)]
            brick_table[offset, voxel] = (target[0] // 4 + 1) * 9 + (target[1] // 4 + 1) * 3 + (target[2] // 4 + 1)
            cell_table[offset, voxel] = target[0] % 4 * 16 + target[1] % 4 * 4 + target[2] % 4
    return (brick_table, cell_table)

def reference(features, mask, rulebook, weight_first, weight_second, cotangent):
    brick_table, cell_table = offset_tables()
    voxel_count = features.shape[0]
    active = mask.astype(jnp.float32)[:, None]
    nearby = rulebook[:, brick_table]
    lookup = jnp.where(nearby >= 0, nearby * 64 + cell_table[None], voxel_count)
    lookup = jnp.transpose(lookup, (1, 0, 2)).reshape(27, voxel_count).astype(jnp.int32)
    offsets = jnp.arange(27, dtype=jnp.int32)
    masked = (features.astype(jnp.float32) * active).astype(jnp.bfloat16)

    def padded_of(source):
        return jnp.concatenate([source, jnp.zeros((1, source.shape[1]), source.dtype)], 0)

    def convolve(source, weight):
        padded = padded_of(source)

        def advance(running, offset):
            picked = jnp.take(padded, lookup[offset], axis=0)
            kernel = lax.dynamic_index_in_dim(weight, offset, 1, keepdims=False)
            return (running + jnp.dot(picked, kernel, preferred_element_type=jnp.float32), None)
        running, unused = lax.scan(advance, jnp.zeros((voxel_count, weight.shape[2]), jnp.float32), offsets)
        return running

    def transposed(gradient, weight):

        def advance(running, offset):
            kernel = lax.dynamic_index_in_dim(weight, offset, 1, keepdims=False)
            contrib = lax.dot_general(gradient, kernel, (((1,), (1,)), ((), ())), preferred_element_type=jnp.float32)
            return (running.at[lookup[offset]].add(contrib), None)
        running, unused = lax.scan(advance, jnp.zeros((voxel_count + 1, weight.shape[0]), jnp.float32), offsets)
        return running[:voxel_count]

    def kernel_grad(source, gradient):
        padded = padded_of(source)

        def advance(carry, offset):
            picked = jnp.take(padded, lookup[offset], axis=0)
            return (carry, lax.dot_general(picked, gradient, (((0,), (0,)), ((), ())), preferred_element_type=jnp.float32))
        unused, stacked = lax.scan(advance, jnp.float32(0.0), offsets)
        return jnp.transpose(stacked, (1, 0, 2))
    first_act = active * convolve(masked, weight_first)
    hidden = jax.nn.silu(first_act).astype(jnp.bfloat16)
    second_act = active * convolve(hidden, weight_second)
    output = second_act.astype(jnp.bfloat16)
    grad_second = (cotangent.astype(jnp.float32) * active).astype(jnp.bfloat16)
    weight_second_grad = kernel_grad(hidden, grad_second)
    hidden_grad = transposed(grad_second, weight_second)
    sigmoid_first = jax.nn.sigmoid(first_act)
    grad_first = (active * hidden_grad * sigmoid_first * (1.0 + first_act * (1.0 - sigmoid_first))).astype(jnp.bfloat16)
    weight_first_grad = kernel_grad(masked, grad_first)
    features_grad = (active * transposed(grad_first, weight_first)).astype(jnp.bfloat16)
    return (output, features_grad, weight_first_grad, weight_second_grad)
```

```python
import functools

import jax
import jax.numpy as jnp
import numpy as np
from jax import lax
from jax.experimental import pallas as pl
from jax.experimental.pallas import tpu as pltpu
from jax.sharding import PartitionSpec as P

HB = 1


direction_steps = (1, 2, -1, -2)


def passed_along(value, axis, by):
    devices = lax.axis_size(axis)
    pairs = [(i, i + by) for i in range(devices) if 0 <= i + by < devices]
    return lax.ppermute(value, axis, pairs)


def offset_tables():
    brick_table = np.zeros((27, 64), np.int32)
    cell_table = np.zeros((27, 64), np.int32)
    for offset in range(27):
        moves = (offset // 9 - 1, offset // 3 % 3 - 1, offset % 3 - 1)
        for voxel in range(64):
            cells = (voxel // 16, voxel // 4 % 4, voxel % 4)
            target = [cells[axis_number] + moves[axis_number] for axis_number in range(3)]
            brick_table[offset, voxel] = (
                (target[0] // 4 + 1) * 9 + (target[1] // 4 + 1) * 3 + (target[2] // 4 + 1)
            )
            cell_table[offset, voxel] = target[0] % 4 * 16 + target[1] % 4 * 4 + target[2] % 4
    return (brick_table, cell_table)


def on_device(features, mask, rulebook, weight_first, weight_second, cotangent):
    brick_table, cell_table = offset_tables()
    bricks = rulebook.shape[0]
    spread = HB
    row_count = features.shape[0]
    halo_rows = 4 * spread * 64
    device_index = lax.axis_index("space")
    owner_device = rulebook // bricks
    within = rulebook % bricks
    sources = device_index - jnp.array(direction_steps, jnp.int32)
    lent_table = (
        jnp.arange(4, dtype=jnp.int32)[:, None] * spread
        + jnp.arange(spread, dtype=jnp.int32)[None, :]
    ) % bricks
    matches = (owner_device[:, :, None, None] == sources[None, None, :, None]) & (
        within[:, :, None, None] == lent_table[None, None]
    )
    numbers = bricks + jnp.arange(4 * spread, dtype=jnp.int32).reshape(4, spread)
    remote = jnp.sum(jnp.where(matches, numbers, 0), axis=(2, 3))
    slot_index = jnp.where(
        rulebook < 0, bricks + 4 * spread, jnp.where(owner_device == device_index, within, remote)
    )
    lookup = slot_index[:, brick_table] * 64 + cell_table[None]
    lookup = jnp.transpose(lookup, (1, 0, 2)).reshape(27, row_count).astype(jnp.int32)
    active = mask.astype(jnp.float32)[:, None]
    masked = (features.astype(jnp.float32) * active).astype(jnp.bfloat16)

    def outgoing(source, position):
        shaped = source.reshape(bricks, 64, source.shape[1])
        return jnp.take(shaped, lent_table[position], axis=0).reshape(spread * 64, source.shape[1])

    def extend(source):
        gathered = lax.all_gather(source, "chan", axis=1, tiled=True)
        blocks = [gathered]
        for position, offset in enumerate(direction_steps):
            blocks.append(passed_along(outgoing(gathered, position), "space", offset))
        blocks.append(jnp.zeros((64, gathered.shape[1]), jnp.bfloat16))
        return jnp.concatenate(blocks, 0)

    def lend_back(own_rows, returned, position):
        shaped = own_rows.reshape(bricks, 64, own_rows.shape[1])
        shaped = shaped.at[lent_table[position]].add(
            returned.reshape(spread, 64, own_rows.shape[1])
        )
        return shaped.reshape(row_count, own_rows.shape[1])

    def settle(running):
        summed = lax.psum_scatter(
            running[: row_count + halo_rows], "chan", scatter_dimension=1, tiled=True
        )
        own_rows = summed[:row_count]
        for position, offset in enumerate(direction_steps):
            block_start = row_count + position * spread * 64
            returned = passed_along(
                summed[block_start : block_start + spread * 64], "space", -offset
            )
            own_rows = lend_back(own_rows, returned, position)
        return own_rows

    def weight_term(extended, gradient):

        def advance(offset):
            picked = jnp.take(extended, lookup[offset], axis=0)
            return lax.dot_general(
                picked, gradient, (((0,), (0,)), ((), ())), preferred_element_type=jnp.float32
            )

        stacked = lax.map(advance, jnp.arange(27, dtype=jnp.int32))
        return jnp.transpose(stacked, (1, 0, 2))

    ext_in = extend(masked)
    table_rows = ext_in.shape[0]
    width = ext_in.shape[1]
    initial = jnp.zeros((row_count, weight_first.shape[2]), jnp.float32)
    segment = lax.all_gather(weight_first, "space", axis=0, tiled=True)
    columns = ext_in

    def advance(offset, running):
        picked = jnp.take(columns, lookup[offset], axis=0)
        kernel = lax.dynamic_index_in_dim(segment, offset, 1, keepdims=False)
        return running + jnp.dot(picked, kernel, preferred_element_type=jnp.float32)

    first_act = active * lax.fori_loop(0, 27, advance, initial)
    hidden = jax.nn.silu(first_act).astype(jnp.bfloat16)
    ext_hidden = extend(hidden)
    second_whole = lax.all_gather(weight_second, "space", axis=0, tiled=True)

    def forward_step(offset, running):
        picked = jnp.take(ext_hidden, lookup[offset], axis=0)
        kernel = lax.dynamic_index_in_dim(second_whole, offset, 1, keepdims=False)
        return running + jnp.dot(picked, kernel, preferred_element_type=jnp.float32)

    second_act = active * lax.fori_loop(
        0, 27, forward_step, jnp.zeros((row_count, second_whole.shape[2]), jnp.float32)
    )
    output = second_act.astype(jnp.bfloat16)
    grad_second = (cotangent.astype(jnp.float32) * active).astype(jnp.bfloat16)
    weight_second_grad = lax.psum_scatter(
        weight_term(ext_hidden, grad_second), "space", scatter_dimension=0, tiled=True
    )

    def backward_step(offset, running):
        kernel = lax.dynamic_index_in_dim(second_whole, offset, 1, keepdims=False)
        contrib = lax.dot_general(
            grad_second, kernel, (((1,), (1,)), ((), ())), preferred_element_type=jnp.float32
        )
        return running.at[lookup[offset]].add(contrib)

    hidden_grad = settle(
        lax.fori_loop(0, 27, backward_step, jnp.zeros((table_rows, width), jnp.float32))
    )
    sigmoid_first = jax.nn.sigmoid(first_act)
    grad_first = (
        active * hidden_grad * sigmoid_first * (1.0 + first_act * (1.0 - sigmoid_first))
    ).astype(jnp.bfloat16)
    weight_first_grad = lax.psum_scatter(
        weight_term(ext_in, grad_first), "space", scatter_dimension=0, tiled=True
    )

    def add_back(running, segment):
        columns = running

        def advance(offset, current):
            kernel = lax.dynamic_index_in_dim(segment, offset, 1, keepdims=False)
            contrib = lax.dot_general(
                grad_first, kernel, (((1,), (1,)), ((), ())), preferred_element_type=jnp.float32
            )
            return current.at[lookup[offset]].add(contrib)

        columns = lax.fori_loop(0, 27, advance, columns)
        return columns

    running = add_back(
        jnp.zeros((table_rows, width), jnp.float32),
        lax.all_gather(weight_first, "space", axis=0, tiled=True),
    )
    features_grad = (active * settle(running)).astype(jnp.bfloat16)
    return (output, features_grad, weight_first_grad, weight_second_grad)


RULE, ROWS1, GRAD2, SUM1, BACK2, ROWS2, GRAD1, SUM2, BACK1 = range(9)
EDGE = 6
CELLS = EDGE**3
HALF = 64
MESH = pl.DeviceIdType.MESH


def margin_tables(bricks):
    spot = np.arange(EDGE)
    step, local = (spot - 1) // 4 + 1, (spot - 1) % 4
    number = 9 * step[:, None, None] + 3 * step[None, :, None] + step[None, None, :]
    cell = 16 * local[:, None, None] + 4 * local[None, :, None] + local[None, None, :]
    return number.reshape(-1), cell.reshape(-1)


def low_lanes(shape):
    return lax.broadcasted_iota(jnp.int32, shape, len(shape) - 1) < HALF


def turned(value):
    return pltpu.roll(value, HALF, 1)


def halves_packed(value):
    upper, lower = value[:64], value[64:]
    low = low_lanes(upper.shape)
    return (
        jnp.where(low, upper, turned(lower)),
        jnp.where(low, turned(upper), lower),
    )


def still_kernel(
    n_s, n_c, table, features, mask, rule, first, second, cotangent,
    output, features_grad, first_grad, second_grad,
    rule_src, rule_buf, rows1_src, rows1_buf, rows2_src, rows2_buf,
    grad2_src, grad2_buf, grad1_src, grad1_buf, sum1_src, sum1_buf, sum2_src, sum2_buf,
    back2_src, back2_buf, back1_src, back1_buf,
    pick, pick_t, order_t, wide1, wide2, margin, folded, ordered2, ordered1, running, kept_act,
    send, recv,
):
    me_s, me_c = lax.axis_index("space"), lax.axis_index("chan")
    bricks, rows = 2 * n_s, 128 * n_s
    f32, bf16 = jnp.float32, jnp.bfloat16

    def is_me(s, c):
        return jnp.logical_and(s == me_s, c == me_c)

    def remote(kind, src, buf, order, slot, s, c):
        return pltpu.make_async_remote_copy(
            src_ref=src, dst_ref=buf.at[slot], send_sem=send.at[kind, order],
            recv_sem=recv.at[kind, slot], device_id=(s, c), device_id_type=MESH,
        )

    def along(kind, src_of, buf):
        for k in range(1, n_s):
            s = lax.rem(me_s + k, n_s)
            yield remote(kind, src_of(s), buf, k, me_s, s, me_c), remote(
                kind, src_of(s), buf, k, s, s, me_c
            )

    def start_along(kind, src_of, buf):
        for out, _ in along(kind, src_of, buf):
            out.start()

    def wait_along(kind, src_of, buf):
        for _, come in along(kind, src_of, buf):
            come.wait_recv()

    def sent_along(kind, src_of, buf):
        for out, _ in along(kind, src_of, buf):
            out.wait_send()

    def spread(kind, src, buf, act):
        for h in range(2):
            for c in range(n_c):
                s = 2 * me_c + h

                @pl.when(jnp.logical_not(is_me(s, c)))
                def _():
                    act(remote(kind, src.at[h], buf, h * n_c + c, me_s, s, c))

    def spread_wait(kind, src, buf):
        for s in range(n_s):

            @pl.when(jnp.logical_not(is_me(s, me_s // 2)))
            def _():
                remote(kind, src.at[0], buf, 0, s, s, me_s // 2).wait_recv()

    def spread_start(kind, src, buf):
        for h in range(2):

            @pl.when(me_s == 2 * me_c + h)
            def _():
                buf[me_s] = src[h]

        spread(kind, src, buf, lambda copy: copy.start())

    def owners(kind, src, buf, act):
        slot = (me_s % 2) * n_c + me_c
        for s in range(n_s):

            @pl.when(jnp.logical_not(is_me(s, me_s // 2)))
            def _():
                act(remote(kind, src.at[s], buf, s, slot, s, me_s // 2))

    def owners_start(kind, src, buf):
        @pl.when(me_s // 2 == me_c)
        def _():
            buf[(me_s % 2) * n_c + me_c] = src[me_s]

        owners(kind, src, buf, lambda copy: copy.start())

    def owners_wait(kind, src, buf):
        for h in range(2):
            for c in range(n_c):
                s = 2 * me_c + h

                @pl.when(jnp.logical_not(is_me(s, c)))
                def _():
                    remote(kind, src.at[0], buf, 0, h * n_c + c, s, c).wait_recv()

    barrier = pltpu.get_barrier_semaphore()

    def greet(s, c):
        pl.semaphore_signal(barrier, inc=1, device_id=(s, c), device_id_type=MESH)

    for k in range(1, n_s):
        greet(lax.rem(me_s + k, n_s), me_c)
    for s in range(n_s):

        @pl.when(jnp.logical_not(is_me(s, me_s // 2)))
        def _():
            greet(s, me_s // 2)

    for h in range(2):
        for c in range(n_c):

            @pl.when(jnp.logical_not(is_me(2 * me_c + h, c)))
            def _():
                greet(2 * me_c + h, c)

    square = (128, 128)
    diagonal = lax.broadcasted_iota(jnp.int32, square, 0) == lax.broadcasted_iota(jnp.int32, square, 1)
    active = jnp.sum(jnp.where(diagonal, mask[...].astype(f32), 0.0), axis=1, keepdims=True)
    masked = features[...].astype(f32) * active
    for h, part in enumerate(halves_packed(masked)):
        rows1_src[h] = part.astype(bf16)
    grad2 = (cotangent[...].astype(f32) * active).astype(bf16)
    grad2_src[...] = grad2
    grad2_buf[me_s] = grad2
    rule_src[...] = jnp.zeros(rule_src.shape, jnp.int32)
    rule_src[0:2, 0:27] = rule[...]
    place = lax.broadcasted_iota(jnp.int32, (bricks, 128), 0)
    own_rule = jnp.where(place == 2 * me_s, rule_src[0:1, :], 0) + jnp.where(
        place == 2 * me_s + 1, rule_src[1:2, :], 0
    )
    rule_src[...] = own_rule
    rule_buf[me_s] = own_rule

    greeted = n_s - 1 + n_s + 2 * n_c - 2 * jnp.where(me_s // 2 == me_c, 1, 0)
    pl.semaphore_wait(barrier, greeted)
    start_along(RULE, lambda s: rule_src, rule_buf)
    spread_start(ROWS1, rows1_src, rows1_buf)
    start_along(GRAD2, lambda s: grad2_src, grad2_buf)

    lane = lax.broadcasted_iota(jnp.int32, (16, rows), 1)
    natural = (lane % bricks) * 64 + lane // bricks
    deep = lax.broadcasted_iota(jnp.int32, (16, rows), 0)

    def order_step(r, carry):
        at = pl.multiple_of(r * 16, 16)
        order_t[pl.ds(at, 16), :] = jnp.where(deep + at == natural, 1.0, 0.0).astype(bf16)
        return carry

    lax.fori_loop(0, rows // 16, order_step, 0)

    wait_along(RULE, lambda s: rule_src, rule_buf)
    whole_rule = rule_buf[0]
    for s in range(1, n_s):
        whole_rule = whole_rule + rule_buf[s]
    numbers, cells = margin_tables(bricks)
    flat = lax.broadcasted_iota(jnp.int32, (bricks, rows), 1)
    shifted = {}
    for e in range(CELLS):
        c = int(numbers[e])
        if c not in shifted:
            shifted[c] = jnp.broadcast_to(whole_rule[:, c : c + 1] * 64, (bricks, 128))
    for e in range(CELLS):
        target = shifted[int(numbers[e])] + int(cells[e])
        for part in range(rows // 128):
            pick[e * bricks : (e + 1) * bricks, part * 128 : part * 128 + 128] = jnp.where(
                flat[:, :128] + part * 128 == target, 1.0, 0.0
            ).astype(bf16)
    numbers_row, cells_row = table[0:1, :], table[1:2, :]
    depth = lax.broadcasted_iota(jnp.int32, (128, CELLS * bricks), 0)
    chosen = jnp.where(depth == numbers_row, 1.0, 0.0).astype(bf16)
    spots = jnp.dot(whole_rule.astype(f32).astype(bf16), chosen, preferred_element_type=f32)
    brick_at = lax.broadcasted_iota(jnp.int32, spots.shape, 0)
    brick_row = table[2:3, :]
    found = jnp.sum(jnp.where(brick_at == brick_row, spots, 0.0), axis=0, keepdims=True)
    found = found.astype(jnp.int32) * 64 + cells_row
    tall = lax.broadcasted_iota(jnp.int32, (16, CELLS * bricks), 0)

    def pick_step(r, carry):
        at = pl.multiple_of(r * 16, 16)
        pick_t[pl.ds(at, 16), :] = jnp.where(tall + at == found, 1.0, 0.0).astype(bf16)
        return carry

    lax.fori_loop(0, rows // 16, pick_step, 0)

    slab = EDGE * EDGE * bricks

    def widen(buf, wide):
        parts = []
        for s in range(n_s):
            block = buf[s].astype(f32)
            back = turned(block)
            low = low_lanes(block.shape)
            parts.append(jnp.where(low, block, back))
            parts.append(jnp.where(low, back, block))
        doubled = jnp.concatenate(parts, 0).astype(bf16)

        def step(i, carry):
            at = pl.multiple_of(i * slab, slab)
            got = jnp.dot(pick[pl.ds(at, slab), :], doubled, preferred_element_type=f32)
            got = got.reshape(EDGE, EDGE, bricks, 128)
            after = jnp.concatenate([got[:, 1:], got[:, EDGE - 1 :]], 1)
            wide[i] = jnp.where(low_lanes(got.shape), got, after).astype(bf16)
            return carry

        lax.fori_loop(0, EDGE, step, 0)

    def taps(wide, i, depth_i, dy):
        chunk = depth_i * 16 * bricks
        near = wide[pl.ds(i, depth_i), pl.ds(dy, 4), 0:4].reshape(chunk, 128)
        far = wide[pl.ds(i, depth_i), pl.ds(dy, 4), 2:6].reshape(chunk, 128)
        return jnp.concatenate([near, far], 1)

    def convolve(wide, weight, target, buf):
        chunk = 16 * bricks

        def step(i, carry):
            total = jnp.zeros((chunk, 128), f32)
            for q in range(9):
                total = total + jnp.dot(
                    taps(wide, i + q // 3, 1, q % 3), weight[q], preferred_element_type=f32
                )
            running[pl.ds(pl.multiple_of(i * chunk, chunk), chunk), :] = total.astype(bf16)
            return carry

        lax.fori_loop(0, 4, step, 0)
        for s in range(n_s):
            block = jnp.dot(
                order_t[s * 128 : (s + 1) * 128, :], running[...], preferred_element_type=f32
            ).astype(bf16)
            target[s] = block
        buf[me_s] = target[me_s]

    def reorder(buf, ordered):
        whole = buf[...].reshape(rows, 128)
        for i in range(4):
            matrix = jnp.concatenate(
                [
                    pick[
                        (((i + 1) * EDGE + j + 1) * EDGE + 1) * bricks : (
                            ((i + 1) * EDGE + j + 1) * EDGE + 5
                        )
                        * bricks,
                        :,
                    ]
                    for j in range(4)
                ],
                0,
            )
            ordered[i * 16 * bricks : (i + 1) * 16 * bricks, :] = jnp.dot(
                matrix, whole, preferred_element_type=f32
            ).astype(bf16)

    def transposed(ordered, weight, target):
        margin[...] = jnp.zeros(margin.shape, f32)
        chunk = 16 * bricks

        def step(q, carry):
            dx, dy = q // 3, q % 3
            kernel = weight[q]
            for i in range(4):
                part = lax.dot_general(
                    ordered[i * chunk : (i + 1) * chunk, :], kernel,
                    (((1,), (1,)), ((), ())), preferred_element_type=f32,
                )
                near = part[:, :128].reshape(1, 4, 4, bricks, 128)
                far = part[:, 128:].reshape(1, 4, 4, bricks, 128)
                margin[pl.ds(i + dx, 1), pl.ds(dy, 4), 0:4] += near
                margin[pl.ds(i + dx, 1), pl.ds(dy, 4), 2:6] += far
            return carry

        lax.fori_loop(0, 9, step, 0)

        def fold(i, carry):
            value = margin[i]
            before = jnp.concatenate([jnp.zeros_like(value[:, :1]), value[:, : EDGE - 1]], 1)
            both = jnp.where(low_lanes(value.shape), value, before).reshape(slab, 128)
            folded[pl.ds(pl.multiple_of(i * slab, slab), slab), :] = (both + turned(both)).astype(bf16)
            return carry

        lax.fori_loop(0, EDGE, fold, 0)

        def back(s, carry):
            at = pl.multiple_of(s * 128, 128)
            got = jnp.dot(pick_t[pl.ds(at, 128), :], folded[...], preferred_element_type=f32)
            upper, lower = got[:64], got[64:]
            target[s] = jnp.where(low_lanes(upper.shape), upper, lower).astype(bf16)
            return carry

        lax.fori_loop(0, n_s, back, 0)

    def kernel_grad(wide, ordered, target):
        def step(q, carry):
            target[q] = lax.dot_general(
                taps(wide, q // 3, 4, q % 3), ordered[...],
                (((0,), (0,)), ((), ())), preferred_element_type=f32,
            )
            return carry

        lax.fori_loop(0, 9, step, 0)

    def summed(buf):
        total = buf[0].astype(f32)
        for s in range(1, n_s):
            total = total + buf[s].astype(f32)
        return total

    def returned(buf):
        sums = []
        for h in range(2):
            total = buf[h * n_c].astype(f32)
            for c in range(1, n_c):
                total = total + buf[h * n_c + c].astype(f32)
            sums.append(total)
        low = low_lanes(sums[0].shape)
        return jnp.concatenate(
            [
                jnp.where(low, sums[0], turned(sums[1])),
                jnp.where(low, turned(sums[0]), sums[1]),
            ],
            0,
        )

    spread_wait(ROWS1, rows1_src, rows1_buf)
    widen(rows1_buf, wide1)
    convolve(wide1, first, sum1_src, sum1_buf)
    start_along(SUM1, lambda s: sum1_src.at[s], sum1_buf)
    wait_along(GRAD2, lambda s: grad2_src, grad2_buf)
    reorder(grad2_buf, ordered2)
    transposed(ordered2, second, back2_src)
    owners_start(BACK2, back2_src, back2_buf)

    wait_along(SUM1, lambda s: sum1_src.at[s], sum1_buf)
    act = active * summed(sum1_buf)
    hidden = act * jax.nn.sigmoid(act)
    for h, part in enumerate(halves_packed(hidden)):
        rows2_src[h] = part.astype(bf16)
    spread_start(ROWS2, rows2_src, rows2_buf)
    kept_act[...] = act

    owners_wait(BACK2, back2_src, back2_buf)
    act = kept_act[...]
    gate = jax.nn.sigmoid(act)
    grad1 = (active * returned(back2_buf) * gate * (1.0 + act * (1.0 - gate))).astype(bf16)
    grad1_src[...] = grad1
    grad1_buf[me_s] = grad1
    start_along(GRAD1, lambda s: grad1_src, grad1_buf)

    spread_wait(ROWS2, rows2_src, rows2_buf)
    widen(rows2_buf, wide2)
    convolve(wide2, second, sum2_src, sum2_buf)
    start_along(SUM2, lambda s: sum2_src.at[s], sum2_buf)
    wait_along(GRAD1, lambda s: grad1_src, grad1_buf)
    reorder(grad1_buf, ordered1)
    transposed(ordered1, first, back1_src)
    owners_start(BACK1, back1_src, back1_buf)

    kernel_grad(wide2, ordered2, second_grad)
    kernel_grad(wide1, ordered1, first_grad)

    wait_along(SUM2, lambda s: sum2_src.at[s], sum2_buf)
    output[...] = active * summed(sum2_buf)
    owners_wait(BACK1, back1_src, back1_buf)
    features_grad[...] = active * returned(back1_buf)

    sent_along(RULE, lambda s: rule_src, rule_buf)
    sent_along(GRAD2, lambda s: grad2_src, grad2_buf)
    sent_along(GRAD1, lambda s: grad1_src, grad1_buf)
    sent_along(SUM1, lambda s: sum1_src.at[s], sum1_buf)
    sent_along(SUM2, lambda s: sum2_src.at[s], sum2_buf)
    spread(ROWS1, rows1_src, rows1_buf, lambda copy: copy.wait_send())
    spread(ROWS2, rows2_src, rows2_buf, lambda copy: copy.wait_send())
    owners(BACK2, back2_src, back2_buf, lambda copy: copy.wait_send())
    owners(BACK1, back1_src, back1_buf, lambda copy: copy.wait_send())


def still_weights(n_s, n_c, features, mask, rulebook, weight_first, weight_second, cotangent):
    bricks, rows = 2 * n_s, 128 * n_s
    numbers, cells = margin_tables(bricks)
    table = np.zeros((8, CELLS * bricks), np.int32)
    table[0] = np.repeat(numbers, bricks)
    table[1] = np.repeat(cells, bricks)
    table[2] = np.tile(np.arange(bricks), CELLS)
    f32, bf16 = jnp.float32, jnp.bfloat16

    def stacked(weight):
        moved = jnp.transpose(weight, (1, 0, 2)).reshape(9, 3 * 64, 128)
        return jnp.pad(moved, ((0, 0), (0, 64), (0, 0)))

    def buffers(shape, kind, sources=None):
        return [pltpu.VMEM(sources or shape, kind), pltpu.VMEM(shape, kind)]

    wide = (EDGE, EDGE, EDGE, bricks, 128)
    packed, square = (n_s, 64, 128), (n_s, 128, 128)
    scratch = (
        buffers((n_s, bricks, 128), jnp.int32, (bricks, 128))
        + buffers(packed, bf16, (2, 64, 128)) * 2
        + buffers(square, bf16, (128, 128)) * 2
        + buffers(square, bf16) * 2
        + buffers(packed, bf16) * 2
        + [
            pltpu.VMEM((CELLS * bricks, rows), bf16),
            pltpu.VMEM((rows, CELLS * bricks), bf16),
            pltpu.VMEM((rows, rows), bf16),
            pltpu.VMEM(wide, bf16),
            pltpu.VMEM(wide, bf16),
            pltpu.VMEM(wide, f32),
            pltpu.VMEM((CELLS * bricks, 128), bf16),
            pltpu.VMEM((rows, 128), bf16),
            pltpu.VMEM((rows, 128), bf16),
            pltpu.VMEM((rows, 128), bf16),
            pltpu.VMEM((128, 128), f32),
            pltpu.SemaphoreType.DMA((9, max(n_s, 2 * n_c))),
            pltpu.SemaphoreType.DMA((9, max(n_s, 2 * n_c))),
        ]
    )
    output, features_grad, first_grad, second_grad = pl.pallas_call(
        functools.partial(still_kernel, n_s, n_c),
        out_shape=[jax.ShapeDtypeStruct((128, 128), f32)] * 2
        + [jax.ShapeDtypeStruct((9, 256, 128), f32)] * 2,
        in_specs=[pl.BlockSpec(memory_space=pltpu.VMEM)] * 7,
        out_specs=[pl.BlockSpec(memory_space=pltpu.VMEM)] * 4,
        scratch_shapes=scratch,
        compiler_params=pltpu.CompilerParams(
            collective_id=0, has_side_effects=True, vmem_limit_bytes=56 * 2**20
        ),
    )(
        table, features, mask.reshape(1, 128), rulebook,
        stacked(weight_first), stacked(weight_second), cotangent,
    )

    def unstacked(grad):
        return jnp.transpose(grad[:, : 3 * 64].reshape(27, 64, 128), (1, 0, 2))

    return (
        output.astype(bf16), features_grad.astype(bf16), unstacked(first_grad), unstacked(second_grad),
    )


def solution(mesh):
    n_space, n_chan = mesh.shape["space"], mesh.shape["chan"]
    body = on_device
    if n_space == 2 * n_chan and n_space <= 8:
        body = functools.partial(still_weights, n_space, n_chan)
    placed = (
        P("space", "chan"),
        P("space"),
        P("space", None),
        P("space", None, "chan"),
        P("space", None, "chan"),
        P("space", "chan"),
    )
    return jax.shard_map(
        body,
        mesh=mesh,
        in_specs=placed,
        out_specs=(
            P("space", "chan"),
            P("space", "chan"),
            P("space", None, "chan"),
            P("space", None, "chan"),
        ),
        check_vma=False,
    )
```

```python
import functools

import jax
import jax.numpy as jnp
import numpy as np
from jax import lax
from jax.experimental import pallas as pl
from jax.experimental.pallas import tpu as pltpu
from jax.sharding import PartitionSpec as P

HB = 1


direction_steps = (1, 2, -1, -2)


def passed_along(value, axis, by):
    devices = lax.axis_size(axis)
    pairs = [(i, i + by) for i in range(devices) if 0 <= i + by < devices]
    return lax.ppermute(value, axis, pairs)


def offset_tables():
    brick_table = np.zeros((27, 64), np.int32)
    cell_table = np.zeros((27, 64), np.int32)
    for offset in range(27):
        moves = (offset // 9 - 1, offset // 3 % 3 - 1, offset % 3 - 1)
        for voxel in range(64):
            cells = (voxel // 16, voxel // 4 % 4, voxel % 4)
            target = [cells[axis_number] + moves[axis_number] for axis_number in range(3)]
            brick_table[offset, voxel] = (
                (target[0] // 4 + 1) * 9 + (target[1] // 4 + 1) * 3 + (target[2] // 4 + 1)
            )
            cell_table[offset, voxel] = target[0] % 4 * 16 + target[1] % 4 * 4 + target[2] % 4
    return (brick_table, cell_table)


def on_device(features, mask, rulebook, weight_first, weight_second, cotangent):
    brick_table, cell_table = offset_tables()
    bricks = rulebook.shape[0]
    spread = HB
    row_count = features.shape[0]
    halo_rows = 4 * spread * 64
    device_index = lax.axis_index("space")
    owner_device = rulebook // bricks
    within = rulebook % bricks
    sources = device_index - jnp.array(direction_steps, jnp.int32)
    lent_table = (
        jnp.arange(4, dtype=jnp.int32)[:, None] * spread
        + jnp.arange(spread, dtype=jnp.int32)[None, :]
    ) % bricks
    matches = (owner_device[:, :, None, None] == sources[None, None, :, None]) & (
        within[:, :, None, None] == lent_table[None, None]
    )
    numbers = bricks + jnp.arange(4 * spread, dtype=jnp.int32).reshape(4, spread)
    remote = jnp.sum(jnp.where(matches, numbers, 0), axis=(2, 3))
    slot_index = jnp.where(
        rulebook < 0, bricks + 4 * spread, jnp.where(owner_device == device_index, within, remote)
    )
    lookup = slot_index[:, brick_table] * 64 + cell_table[None]
    lookup = jnp.transpose(lookup, (1, 0, 2)).reshape(27, row_count).astype(jnp.int32)
    active = mask.astype(jnp.float32)[:, None]
    masked = (features.astype(jnp.float32) * active).astype(jnp.bfloat16)

    def outgoing(source, position):
        shaped = source.reshape(bricks, 64, source.shape[1])
        return jnp.take(shaped, lent_table[position], axis=0).reshape(spread * 64, source.shape[1])

    def extend(source):
        gathered = lax.all_gather(source, "chan", axis=1, tiled=True)
        blocks = [gathered]
        for position, offset in enumerate(direction_steps):
            blocks.append(passed_along(outgoing(gathered, position), "space", offset))
        blocks.append(jnp.zeros((64, gathered.shape[1]), jnp.bfloat16))
        return jnp.concatenate(blocks, 0)

    def lend_back(own_rows, returned, position):
        shaped = own_rows.reshape(bricks, 64, own_rows.shape[1])
        shaped = shaped.at[lent_table[position]].add(
            returned.reshape(spread, 64, own_rows.shape[1])
        )
        return shaped.reshape(row_count, own_rows.shape[1])

    def settle(running):
        summed = lax.psum_scatter(
            running[: row_count + halo_rows], "chan", scatter_dimension=1, tiled=True
        )
        own_rows = summed[:row_count]
        for position, offset in enumerate(direction_steps):
            block_start = row_count + position * spread * 64
            returned = passed_along(
                summed[block_start : block_start + spread * 64], "space", -offset
            )
            own_rows = lend_back(own_rows, returned, position)
        return own_rows

    def weight_term(extended, gradient):

        def advance(offset):
            picked = jnp.take(extended, lookup[offset], axis=0)
            return lax.dot_general(
                picked, gradient, (((0,), (0,)), ((), ())), preferred_element_type=jnp.float32
            )

        stacked = lax.map(advance, jnp.arange(27, dtype=jnp.int32))
        return jnp.transpose(stacked, (1, 0, 2))

    ext_in = extend(masked)
    table_rows = ext_in.shape[0]
    width = ext_in.shape[1]
    initial = jnp.zeros((row_count, weight_first.shape[2]), jnp.float32)
    segment = lax.all_gather(weight_first, "space", axis=0, tiled=True)
    columns = ext_in

    def advance(offset, running):
        picked = jnp.take(columns, lookup[offset], axis=0)
        kernel = lax.dynamic_index_in_dim(segment, offset, 1, keepdims=False)
        return running + jnp.dot(picked, kernel, preferred_element_type=jnp.float32)

    first_act = active * lax.fori_loop(0, 27, advance, initial)
    hidden = jax.nn.silu(first_act).astype(jnp.bfloat16)
    ext_hidden = extend(hidden)
    second_whole = lax.all_gather(weight_second, "space", axis=0, tiled=True)

    def forward_step(offset, running):
        picked = jnp.take(ext_hidden, lookup[offset], axis=0)
        kernel = lax.dynamic_index_in_dim(second_whole, offset, 1, keepdims=False)
        return running + jnp.dot(picked, kernel, preferred_element_type=jnp.float32)

    second_act = active * lax.fori_loop(
        0, 27, forward_step, jnp.zeros((row_count, second_whole.shape[2]), jnp.float32)
    )
    output = second_act.astype(jnp.bfloat16)
    grad_second = (cotangent.astype(jnp.float32) * active).astype(jnp.bfloat16)
    weight_second_grad = lax.psum_scatter(
        weight_term(ext_hidden, grad_second), "space", scatter_dimension=0, tiled=True
    )

    def backward_step(offset, running):
        kernel = lax.dynamic_index_in_dim(second_whole, offset, 1, keepdims=False)
        contrib = lax.dot_general(
            grad_second, kernel, (((1,), (1,)), ((), ())), preferred_element_type=jnp.float32
        )
        return running.at[lookup[offset]].add(contrib)

    hidden_grad = settle(
        lax.fori_loop(0, 27, backward_step, jnp.zeros((table_rows, width), jnp.float32))
    )
    sigmoid_first = jax.nn.sigmoid(first_act)
    grad_first = (
        active * hidden_grad * sigmoid_first * (1.0 + first_act * (1.0 - sigmoid_first))
    ).astype(jnp.bfloat16)
    weight_first_grad = lax.psum_scatter(
        weight_term(ext_in, grad_first), "space", scatter_dimension=0, tiled=True
    )

    def add_back(running, segment):
        columns = running

        def advance(offset, current):
            kernel = lax.dynamic_index_in_dim(segment, offset, 1, keepdims=False)
            contrib = lax.dot_general(
                grad_first, kernel, (((1,), (1,)), ((), ())), preferred_element_type=jnp.float32
            )
            return current.at[lookup[offset]].add(contrib)

        columns = lax.fori_loop(0, 27, advance, columns)
        return columns

    running = add_back(
        jnp.zeros((table_rows, width), jnp.float32),
        lax.all_gather(weight_first, "space", axis=0, tiled=True),
    )
    features_grad = (active * settle(running)).astype(jnp.bfloat16)
    return (output, features_grad, weight_first_grad, weight_second_grad)


RULE, ROWS1, GRAD2, SUM1, BACK2, ROWS2, GRAD1, SUM2, BACK1 = range(9)
EDGE = 6
HALF = 64
MESH = pl.DeviceIdType.MESH


def brick_offsets():
    targets, sources = (slice(0, 1), slice(1, 5), slice(5, 6)), (slice(4, 5), slice(1, 5), slice(1, 2))
    counts = {16: 0, 4: 0, 1: 0}
    found = []
    for c in range(27):
        moves = (c // 9, c // 3 % 3, c % 3)
        cells = 4 ** moves.count(1)
        if c != 13:
            found.append(
                (c, cells, counts[cells], tuple(targets[m] for m in moves), tuple(sources[m] for m in moves))
            )
            counts[cells] += 1
    return found


def low_lanes(shape):
    return lax.broadcasted_iota(jnp.int32, shape, len(shape) - 1) < HALF


def turned(value):
    return pltpu.roll(value, HALF, 1)


def halves_packed(value):
    upper, lower = value[:64], value[64:]
    low = low_lanes(upper.shape)
    return (
        jnp.where(low, upper, turned(lower)),
        jnp.where(low, turned(upper), lower),
    )


def still_kernel(
    n_s, n_c, features, mask, rule, first, second, cotangent,
    output, features_grad, first_grad, second_grad,
    rule_src, rule_buf, rows1_src, rows1_buf, rows2_src, rows2_buf,
    grad2_src, grad2_buf, grad1_src, grad1_buf, sum1_src, sum1_buf, sum2_src, sum2_buf,
    back2_src, back2_buf, back1_src, back1_buf,
    faces, edges, corners, order, order_t, raw, wide1, wide2, margin,
    ordered2, ordered1, flipped2, flipped1, running, kept_act, first_stack, second_stack,
    send, recv,
):
    me_s, me_c = lax.axis_index("space"), lax.axis_index("chan")
    bricks, rows = 2 * n_s, 128 * n_s
    f32, bf16 = jnp.float32, jnp.bfloat16

    def is_me(s, c):
        return jnp.logical_and(s == me_s, c == me_c)

    def remote(kind, src, buf, order, slot, s, c):
        return pltpu.make_async_remote_copy(
            src_ref=src, dst_ref=buf.at[slot], send_sem=send.at[kind, order],
            recv_sem=recv.at[kind, slot], device_id=(s, c), device_id_type=MESH,
        )

    def along(kind, src_of, buf):
        for k in range(1, n_s):
            s = lax.rem(me_s + k, n_s)
            yield remote(kind, src_of(s), buf, k, me_s, s, me_c), remote(
                kind, src_of(s), buf, k, s, s, me_c
            )

    def start_along(kind, src_of, buf):
        for out, _ in along(kind, src_of, buf):
            out.start()

    def wait_along(kind, src_of, buf):
        for _, come in along(kind, src_of, buf):
            come.wait_recv()

    def sent_along(kind, src_of, buf):
        for out, _ in along(kind, src_of, buf):
            out.wait_send()

    def spread(kind, src, buf, act):
        for h in range(2):
            for c in range(n_c):
                s = 2 * me_c + h

                @pl.when(jnp.logical_not(is_me(s, c)))
                def _():
                    act(remote(kind, src.at[h], buf, h * n_c + c, me_s, s, c))

    def spread_wait(kind, src, buf):
        for s in range(n_s):

            @pl.when(jnp.logical_not(is_me(s, me_s // 2)))
            def _():
                remote(kind, src.at[0], buf, 0, s, s, me_s // 2).wait_recv()

    def spread_start(kind, src, buf):
        for h in range(2):

            @pl.when(me_s == 2 * me_c + h)
            def _():
                buf[me_s] = src[h]

        spread(kind, src, buf, lambda copy: copy.start())

    def owners(kind, src, buf, act):
        slot = (me_s % 2) * n_c + me_c
        for s in range(n_s):

            @pl.when(jnp.logical_not(is_me(s, me_s // 2)))
            def _():
                act(remote(kind, src.at[s], buf, s, slot, s, me_s // 2))

    def owners_start(kind, src, buf):
        @pl.when(me_s // 2 == me_c)
        def _():
            buf[(me_s % 2) * n_c + me_c] = src[me_s]

        owners(kind, src, buf, lambda copy: copy.start())

    def owners_wait(kind, src, buf):
        for h in range(2):
            for c in range(n_c):
                s = 2 * me_c + h

                @pl.when(jnp.logical_not(is_me(s, c)))
                def _():
                    remote(kind, src.at[0], buf, 0, h * n_c + c, s, c).wait_recv()

    barrier = pltpu.get_barrier_semaphore()

    def greet(s, c):
        pl.semaphore_signal(barrier, inc=1, device_id=(s, c), device_id_type=MESH)

    for k in range(1, n_s):
        greet(lax.rem(me_s + k, n_s), me_c)
    for s in range(n_s):

        @pl.when(jnp.logical_not(is_me(s, me_s // 2)))
        def _():
            greet(s, me_s // 2)

    for h in range(2):
        for c in range(n_c):

            @pl.when(jnp.logical_not(is_me(2 * me_c + h, c)))
            def _():
                greet(2 * me_c + h, c)

    square = (128, 128)
    diagonal = lax.broadcasted_iota(jnp.int32, square, 0) == lax.broadcasted_iota(jnp.int32, square, 1)
    active = jnp.sum(jnp.where(diagonal, mask[...].astype(f32), 0.0), axis=1, keepdims=True)
    masked = features[...].astype(f32) * active
    for h, part in enumerate(halves_packed(masked)):
        rows1_src[h] = part.astype(bf16)
    grad2 = (cotangent[...].astype(f32) * active).astype(bf16)
    grad2_src[...] = grad2
    grad2_buf[me_s] = grad2
    rule_src[...] = jnp.zeros(rule_src.shape, jnp.int32)
    rule_src[0:2, 0:27] = rule[...]
    place = lax.broadcasted_iota(jnp.int32, (bricks, 128), 0)
    own_rule = jnp.where(place == 2 * me_s, rule_src[0:1, :], 0) + jnp.where(
        place == 2 * me_s + 1, rule_src[1:2, :], 0
    )
    rule_src[...] = own_rule
    rule_buf[me_s] = own_rule

    greeted = n_s - 1 + n_s + 2 * n_c - 2 * jnp.where(me_s // 2 == me_c, 1, 0)
    pl.semaphore_wait(barrier, greeted)
    start_along(RULE, lambda s: rule_src, rule_buf)
    spread_start(ROWS1, rows1_src, rows1_buf)
    start_along(GRAD2, lambda s: grad2_src, grad2_buf)

    lane = lax.broadcasted_iota(jnp.int32, (16, rows), 1)
    natural = (lane % bricks) * 64 + lane // bricks
    deep = lax.broadcasted_iota(jnp.int32, (16, rows), 0)

    def order_step(r, carry):
        at = pl.multiple_of(r * 16, 16)
        order_t[pl.ds(at, 16), :] = jnp.where(deep + at == natural, 1.0, 0.0).astype(bf16)
        order[pl.ds(at, 16), :] = jnp.where(deep * 64 + r == lane, 1.0, 0.0).astype(bf16)
        return carry

    lax.fori_loop(0, rows // 16, order_step, 0)
    for weight, stack in ((first, first_stack), (second, second_stack)):
        for q in range(9):
            stack[q, 0:192, :] = weight[3 * q : 3 * q + 3].reshape(192, 128)
            stack[q, 192:256, :] = jnp.zeros((64, 128), bf16)

    wait_along(RULE, lambda s: rule_src, rule_buf)
    whole_rule = rule_buf[0]
    for s in range(1, n_s):
        whole_rule = whole_rule + rule_buf[s]
    whole_rule = jnp.where(whole_rule < 0, -4096, whole_rule)
    which = {16: faces, 4: edges, 1: corners}
    for c, cells, at, _, _ in brick_offsets():
        fed = jnp.broadcast_to(whole_rule[:, c : c + 1], (bricks, 128))
        span = cells * bricks
        for cell in range(cells):
            for part in range(0, span, 128):
                width = min(128, span - part)
                hit = lane[:, :128] + (part - cell * bricks) == fed
                which[cells][at, cell * bricks : (cell + 1) * bricks, part : part + width] = (
                    jnp.where(hit, 1.0, 0.0).astype(bf16)[:, :width]
                )

    slab = EDGE * EDGE * bricks

    def widen(buf, wide):
        parts = []
        for s in range(n_s):
            block = buf[s].astype(f32)
            back = turned(block)
            low = low_lanes(block.shape)
            parts.append(jnp.where(low, block, back))
            parts.append(jnp.where(low, back, block))
        doubled = jnp.concatenate(parts, 0).astype(bf16)

        for i in range(4):
            got = jnp.dot(order[i * 256 : (i + 1) * 256, :], doubled, preferred_element_type=f32)
            raw[i + 1, 1:5, 1:5] = got.reshape(4, 4, bricks, 128).astype(bf16)
        for c, cells, at, target, source in brick_offsets():
            value = raw[source].reshape(cells * bricks, 128)
            got = jnp.dot(which[cells][at], value, preferred_element_type=f32)
            raw[target] = got.astype(bf16).reshape(raw[target].shape)

        def step(i, carry):
            got = raw[i].astype(f32)
            after = jnp.concatenate([got[:, 1:], got[:, EDGE - 1 :]], 1)
            wide[i] = jnp.where(low_lanes(got.shape), got, after).astype(bf16)
            return carry

        lax.fori_loop(0, EDGE, step, 0)

    def taps(wide, i, depth_i, dy):
        chunk = depth_i * 16 * bricks
        near = wide[pl.ds(i, depth_i), pl.ds(dy, 4), 0:4].reshape(chunk, 128)
        far = wide[pl.ds(i, depth_i), pl.ds(dy, 4), 2:6].reshape(chunk, 128)
        return jnp.concatenate([near, far], 1)

    def convolve(wide, weight, target, buf):
        chunk = 16 * bricks

        def step(i, carry):
            total = jnp.zeros((chunk, 128), f32)
            for q in range(9):
                total = total + jnp.dot(
                    taps(wide, i + q // 3, 1, q % 3), weight[q], preferred_element_type=f32
                )
            running[pl.ds(pl.multiple_of(i * chunk, chunk), chunk), :] = total.astype(bf16)
            return carry

        lax.fori_loop(0, 4, step, 0)
        for s in range(n_s):
            block = jnp.dot(
                order_t[s * 128 : (s + 1) * 128, :], running[...], preferred_element_type=f32
            ).astype(bf16)
            target[s] = block
        buf[me_s] = target[me_s]

    def reorder(buf, ordered, flipped):
        whole = buf[...].reshape(rows, 128)
        for i in range(4):
            got = jnp.dot(order[i * 256 : (i + 1) * 256, :], whole, preferred_element_type=f32)
            ordered[i * 256 : (i + 1) * 256, :] = got.astype(bf16)
            flipped[:, i * 256 : (i + 1) * 256] = got.T.astype(bf16)

    def transposed(ordered, weight, target):
        margin[...] = jnp.zeros(margin.shape, f32)
        chunk = 16 * bricks

        def step(q, carry):
            dx, dy = q // 3, q % 3
            kernel = weight[q]
            for i in range(4):
                part = lax.dot_general(
                    ordered[i * chunk : (i + 1) * chunk, :], kernel,
                    (((1,), (1,)), ((), ())), preferred_element_type=f32,
                )
                near = part[:, :128].reshape(1, 4, 4, bricks, 128)
                far = part[:, 128:].reshape(1, 4, 4, bricks, 128)
                margin[pl.ds(i + dx, 1), pl.ds(dy, 4), 0:4] += near
                margin[pl.ds(i + dx, 1), pl.ds(dy, 4), 2:6] += far
            return carry

        lax.fori_loop(0, 9, step, 0)

        def fold(i, carry):
            value = margin[i]
            before = jnp.concatenate([jnp.zeros_like(value[:, :1]), value[:, : EDGE - 1]], 1)
            both = jnp.where(low_lanes(value.shape), value, before).reshape(slab, 128)
            margin[i] = (both + turned(both)).reshape(value.shape)
            return carry

        lax.fori_loop(0, EDGE, fold, 0)
        for c, cells, at, source, owner in brick_offsets():
            value = margin[source].reshape(cells * bricks, 128)
            coarse = value.astype(bf16).astype(f32)
            split = jnp.where(low_lanes(value.shape), coarse, value - coarse).astype(bf16)
            got = lax.dot_general(
                which[cells][at], split, (((0,), (0,)), ((), ())), preferred_element_type=f32
            )
            margin[owner] += (got + turned(got)).reshape(margin[owner].shape)
        running[...] = margin[1:5, 1:5, 1:5].reshape(rows, 128).astype(bf16)

        def back(s, carry):
            at = pl.multiple_of(s * 128, 128)
            got = jnp.dot(order_t[pl.ds(at, 128), :], running[...], preferred_element_type=f32)
            upper, lower = got[:64], got[64:]
            target[s] = jnp.where(low_lanes(upper.shape), upper, lower).astype(bf16)
            return carry

        lax.fori_loop(0, n_s, back, 0)

    def kernel_grad(wide, flipped, target):
        def step(q, carry):
            got = jnp.dot(flipped[...], taps(wide, q // 3, 4, q % 3), preferred_element_type=f32)
            target[pl.ds(3 * q, 3)] = got.T[:192].reshape(3, 64, 128)
            return carry

        lax.fori_loop(0, 9, step, 0)

    def summed(buf):
        total = buf[0].astype(f32)
        for s in range(1, n_s):
            total = total + buf[s].astype(f32)
        return total

    def returned(buf):
        sums = []
        for h in range(2):
            total = buf[h * n_c].astype(f32)
            for c in range(1, n_c):
                total = total + buf[h * n_c + c].astype(f32)
            sums.append(total)
        low = low_lanes(sums[0].shape)
        return jnp.concatenate(
            [
                jnp.where(low, sums[0], turned(sums[1])),
                jnp.where(low, turned(sums[0]), sums[1]),
            ],
            0,
        )

    spread_wait(ROWS1, rows1_src, rows1_buf)
    widen(rows1_buf, wide1)
    convolve(wide1, first_stack, sum1_src, sum1_buf)
    start_along(SUM1, lambda s: sum1_src.at[s], sum1_buf)
    wait_along(GRAD2, lambda s: grad2_src, grad2_buf)
    reorder(grad2_buf, ordered2, flipped2)
    transposed(ordered2, second_stack, back2_src)
    owners_start(BACK2, back2_src, back2_buf)

    wait_along(SUM1, lambda s: sum1_src.at[s], sum1_buf)
    act = active * summed(sum1_buf)
    hidden = act * jax.nn.sigmoid(act)
    for h, part in enumerate(halves_packed(hidden)):
        rows2_src[h] = part.astype(bf16)
    spread_start(ROWS2, rows2_src, rows2_buf)
    kept_act[...] = act

    owners_wait(BACK2, back2_src, back2_buf)
    act = kept_act[...]
    gate = jax.nn.sigmoid(act)
    grad1 = (active * returned(back2_buf) * gate * (1.0 + act * (1.0 - gate))).astype(bf16)
    grad1_src[...] = grad1
    grad1_buf[me_s] = grad1
    start_along(GRAD1, lambda s: grad1_src, grad1_buf)

    spread_wait(ROWS2, rows2_src, rows2_buf)
    widen(rows2_buf, wide2)
    convolve(wide2, second_stack, sum2_src, sum2_buf)
    start_along(SUM2, lambda s: sum2_src.at[s], sum2_buf)
    wait_along(GRAD1, lambda s: grad1_src, grad1_buf)
    reorder(grad1_buf, ordered1, flipped1)
    transposed(ordered1, first_stack, back1_src)
    owners_start(BACK1, back1_src, back1_buf)

    kernel_grad(wide2, flipped2, second_grad)
    kernel_grad(wide1, flipped1, first_grad)

    wait_along(SUM2, lambda s: sum2_src.at[s], sum2_buf)
    output[...] = (active * summed(sum2_buf)).astype(bf16)
    owners_wait(BACK1, back1_src, back1_buf)
    features_grad[...] = (active * returned(back1_buf)).astype(bf16)

    sent_along(RULE, lambda s: rule_src, rule_buf)
    sent_along(GRAD2, lambda s: grad2_src, grad2_buf)
    sent_along(GRAD1, lambda s: grad1_src, grad1_buf)
    sent_along(SUM1, lambda s: sum1_src.at[s], sum1_buf)
    sent_along(SUM2, lambda s: sum2_src.at[s], sum2_buf)
    spread(ROWS1, rows1_src, rows1_buf, lambda copy: copy.wait_send())
    spread(ROWS2, rows2_src, rows2_buf, lambda copy: copy.wait_send())
    owners(BACK2, back2_src, back2_buf, lambda copy: copy.wait_send())
    owners(BACK1, back1_src, back1_buf, lambda copy: copy.wait_send())


def still_weights(n_s, n_c, features, mask, rulebook, weight_first, weight_second, cotangent):
    bricks, rows = 2 * n_s, 128 * n_s
    f32, bf16 = jnp.float32, jnp.bfloat16

    def stacked(weight):
        return jnp.transpose(weight, (1, 0, 2))

    def buffers(shape, kind, sources=None):
        return [pltpu.VMEM(sources or shape, kind), pltpu.VMEM(shape, kind)]

    wide = (EDGE, EDGE, EDGE, bricks, 128)
    packed, square = (n_s, 64, 128), (n_s, 128, 128)
    scratch = (
        buffers((n_s, bricks, 128), jnp.int32, (bricks, 128))
        + buffers(packed, bf16, (2, 64, 128)) * 2
        + buffers(square, bf16, (128, 128)) * 2
        + buffers(square, bf16) * 2
        + buffers(packed, bf16) * 2
        + [
            pltpu.VMEM((6, 256, 256), bf16),
            pltpu.VMEM((12, 64, 64), bf16),
            pltpu.VMEM((8, 16, 16), bf16),
            pltpu.VMEM((rows, rows), bf16),
            pltpu.VMEM((rows, rows), bf16),
            pltpu.VMEM(wide, bf16),
            pltpu.VMEM(wide, bf16),
            pltpu.VMEM(wide, bf16),
            pltpu.VMEM(wide, f32),
            pltpu.VMEM((rows, 128), bf16),
            pltpu.VMEM((rows, 128), bf16),
            pltpu.VMEM((128, rows), bf16),
            pltpu.VMEM((128, rows), bf16),
            pltpu.VMEM((rows, 128), bf16),
            pltpu.VMEM((128, 128), f32),
            pltpu.VMEM((9, 256, 128), bf16),
            pltpu.VMEM((9, 256, 128), bf16),
            pltpu.SemaphoreType.DMA((9, max(n_s, 2 * n_c))),
            pltpu.SemaphoreType.DMA((9, max(n_s, 2 * n_c))),
        ]
    )
    output, features_grad, first_grad, second_grad = pl.pallas_call(
        functools.partial(still_kernel, n_s, n_c),
        out_shape=[jax.ShapeDtypeStruct((128, 128), bf16)] * 2
        + [jax.ShapeDtypeStruct((27, 64, 128), f32)] * 2,
        in_specs=[pl.BlockSpec(memory_space=pltpu.VMEM)] * 6,
        out_specs=[pl.BlockSpec(memory_space=pltpu.VMEM)] * 4,
        scratch_shapes=scratch,
        compiler_params=pltpu.CompilerParams(
            collective_id=0, has_side_effects=True, vmem_limit_bytes=48 * 2**20
        ),
    )(
        features, mask.reshape(1, 128), rulebook,
        stacked(weight_first), stacked(weight_second), cotangent,
    )

    def unstacked(grad):
        return jnp.transpose(grad, (1, 0, 2))

    return (
        output, features_grad, unstacked(first_grad), unstacked(second_grad),
    )


def solution(mesh):
    n_space, n_chan = mesh.shape["space"], mesh.shape["chan"]
    body = on_device
    if n_space == 8 and n_chan == 4:
        body = functools.partial(still_weights, n_space, n_chan)
    placed = (
        P("space", "chan"),
        P("space"),
        P("space", None),
        P("space", None, "chan"),
        P("space", None, "chan"),
        P("space", "chan"),
    )
    return jax.shard_map(
        body,
        mesh=mesh,
        in_specs=placed,
        out_specs=(
            P("space", "chan"),
            P("space", "chan"),
            P("space", None, "chan"),
            P("space", None, "chan"),
        ),
        check_vma=False,
    )
```

```python
import functools

import jax
import jax.numpy as jnp
import numpy as np
from jax import lax
from jax.experimental import pallas as pl
from jax.experimental.pallas import tpu as pltpu
from jax.sharding import PartitionSpec as P

HB = 1


direction_steps = (1, 2, -1, -2)


def passed_along(value, axis, by):
    devices = lax.axis_size(axis)
    pairs = [(i, i + by) for i in range(devices) if 0 <= i + by < devices]
    return lax.ppermute(value, axis, pairs)


def offset_tables():
    brick_table = np.zeros((27, 64), np.int32)
    cell_table = np.zeros((27, 64), np.int32)
    for offset in range(27):
        moves = (offset // 9 - 1, offset // 3 % 3 - 1, offset % 3 - 1)
        for voxel in range(64):
            cells = (voxel // 16, voxel // 4 % 4, voxel % 4)
            target = [cells[axis_number] + moves[axis_number] for axis_number in range(3)]
            brick_table[offset, voxel] = (
                (target[0] // 4 + 1) * 9 + (target[1] // 4 + 1) * 3 + (target[2] // 4 + 1)
            )
            cell_table[offset, voxel] = target[0] % 4 * 16 + target[1] % 4 * 4 + target[2] % 4
    return (brick_table, cell_table)


def on_device(features, mask, rulebook, weight_first, weight_second, cotangent):
    brick_table, cell_table = offset_tables()
    bricks = rulebook.shape[0]
    spread = HB
    row_count = features.shape[0]
    halo_rows = 4 * spread * 64
    device_index = lax.axis_index("space")
    owner_device = rulebook // bricks
    within = rulebook % bricks
    sources = device_index - jnp.array(direction_steps, jnp.int32)
    lent_table = (
        jnp.arange(4, dtype=jnp.int32)[:, None] * spread
        + jnp.arange(spread, dtype=jnp.int32)[None, :]
    ) % bricks
    matches = (owner_device[:, :, None, None] == sources[None, None, :, None]) & (
        within[:, :, None, None] == lent_table[None, None]
    )
    numbers = bricks + jnp.arange(4 * spread, dtype=jnp.int32).reshape(4, spread)
    remote = jnp.sum(jnp.where(matches, numbers, 0), axis=(2, 3))
    slot_index = jnp.where(
        rulebook < 0, bricks + 4 * spread, jnp.where(owner_device == device_index, within, remote)
    )
    lookup = slot_index[:, brick_table] * 64 + cell_table[None]
    lookup = jnp.transpose(lookup, (1, 0, 2)).reshape(27, row_count).astype(jnp.int32)
    active = mask.astype(jnp.float32)[:, None]
    masked = (features.astype(jnp.float32) * active).astype(jnp.bfloat16)

    def outgoing(source, position):
        shaped = source.reshape(bricks, 64, source.shape[1])
        return jnp.take(shaped, lent_table[position], axis=0).reshape(spread * 64, source.shape[1])

    def extend(source):
        gathered = lax.all_gather(source, "chan", axis=1, tiled=True)
        blocks = [gathered]
        for position, offset in enumerate(direction_steps):
            blocks.append(passed_along(outgoing(gathered, position), "space", offset))
        blocks.append(jnp.zeros((64, gathered.shape[1]), jnp.bfloat16))
        return jnp.concatenate(blocks, 0)

    def lend_back(own_rows, returned, position):
        shaped = own_rows.reshape(bricks, 64, own_rows.shape[1])
        shaped = shaped.at[lent_table[position]].add(
            returned.reshape(spread, 64, own_rows.shape[1])
        )
        return shaped.reshape(row_count, own_rows.shape[1])

    def settle(running):
        summed = lax.psum_scatter(
            running[: row_count + halo_rows], "chan", scatter_dimension=1, tiled=True
        )
        own_rows = summed[:row_count]
        for position, offset in enumerate(direction_steps):
            block_start = row_count + position * spread * 64
            returned = passed_along(
                summed[block_start : block_start + spread * 64], "space", -offset
            )
            own_rows = lend_back(own_rows, returned, position)
        return own_rows

    def weight_term(extended, gradient):

        def advance(offset):
            picked = jnp.take(extended, lookup[offset], axis=0)
            return lax.dot_general(
                picked, gradient, (((0,), (0,)), ((), ())), preferred_element_type=jnp.float32
            )

        stacked = lax.map(advance, jnp.arange(27, dtype=jnp.int32))
        return jnp.transpose(stacked, (1, 0, 2))

    ext_in = extend(masked)
    table_rows = ext_in.shape[0]
    width = ext_in.shape[1]
    initial = jnp.zeros((row_count, weight_first.shape[2]), jnp.float32)
    segment = lax.all_gather(weight_first, "space", axis=0, tiled=True)
    columns = ext_in

    def advance(offset, running):
        picked = jnp.take(columns, lookup[offset], axis=0)
        kernel = lax.dynamic_index_in_dim(segment, offset, 1, keepdims=False)
        return running + jnp.dot(picked, kernel, preferred_element_type=jnp.float32)

    first_act = active * lax.fori_loop(0, 27, advance, initial)
    hidden = jax.nn.silu(first_act).astype(jnp.bfloat16)
    ext_hidden = extend(hidden)
    second_whole = lax.all_gather(weight_second, "space", axis=0, tiled=True)

    def forward_step(offset, running):
        picked = jnp.take(ext_hidden, lookup[offset], axis=0)
        kernel = lax.dynamic_index_in_dim(second_whole, offset, 1, keepdims=False)
        return running + jnp.dot(picked, kernel, preferred_element_type=jnp.float32)

    second_act = active * lax.fori_loop(
        0, 27, forward_step, jnp.zeros((row_count, second_whole.shape[2]), jnp.float32)
    )
    output = second_act.astype(jnp.bfloat16)
    grad_second = (cotangent.astype(jnp.float32) * active).astype(jnp.bfloat16)
    weight_second_grad = lax.psum_scatter(
        weight_term(ext_hidden, grad_second), "space", scatter_dimension=0, tiled=True
    )

    def backward_step(offset, running):
        kernel = lax.dynamic_index_in_dim(second_whole, offset, 1, keepdims=False)
        contrib = lax.dot_general(
            grad_second, kernel, (((1,), (1,)), ((), ())), preferred_element_type=jnp.float32
        )
        return running.at[lookup[offset]].add(contrib)

    hidden_grad = settle(
        lax.fori_loop(0, 27, backward_step, jnp.zeros((table_rows, width), jnp.float32))
    )
    sigmoid_first = jax.nn.sigmoid(first_act)
    grad_first = (
        active * hidden_grad * sigmoid_first * (1.0 + first_act * (1.0 - sigmoid_first))
    ).astype(jnp.bfloat16)
    weight_first_grad = lax.psum_scatter(
        weight_term(ext_in, grad_first), "space", scatter_dimension=0, tiled=True
    )

    def add_back(running, segment):
        columns = running

        def advance(offset, current):
            kernel = lax.dynamic_index_in_dim(segment, offset, 1, keepdims=False)
            contrib = lax.dot_general(
                grad_first, kernel, (((1,), (1,)), ((), ())), preferred_element_type=jnp.float32
            )
            return current.at[lookup[offset]].add(contrib)

        columns = lax.fori_loop(0, 27, advance, columns)
        return columns

    running = add_back(
        jnp.zeros((table_rows, width), jnp.float32),
        lax.all_gather(weight_first, "space", axis=0, tiled=True),
    )
    features_grad = (active * settle(running)).astype(jnp.bfloat16)
    return (output, features_grad, weight_first_grad, weight_second_grad)


RULE, ROWS1, GRAD2, SUM1, PART2, BACK2, ROWS2, GRAD1, SUM2, PART1, BACK1 = range(11)
EDGE = 6
HALF = 64
MESH = pl.DeviceIdType.MESH


def brick_offsets():
    targets, sources = (slice(0, 1), slice(1, 5), slice(5, 6)), (slice(4, 5), slice(1, 5), slice(1, 2))
    counts = {16: 0, 4: 0, 1: 0}
    found = []
    for c in range(27):
        moves = (c // 9, c // 3 % 3, c % 3)
        cells = 4 ** moves.count(1)
        if c != 13:
            found.append(
                (c, cells, counts[cells], tuple(targets[m] for m in moves), tuple(sources[m] for m in moves))
            )
            counts[cells] += 1
    return found


def low_lanes(shape):
    return lax.broadcasted_iota(jnp.int32, shape, len(shape) - 1) < HALF


def turned(value):
    return pltpu.roll(value, HALF, 1)


def halves_packed(value):
    upper, lower = value[:64], value[64:]
    low = low_lanes(upper.shape)
    return (
        jnp.where(low, upper, turned(lower)),
        jnp.where(low, turned(upper), lower),
    )


def still_kernel(
    n_s, n_c, features_hbm, mask_hbm, rule_hbm, first_hbm, second_hbm, cotangent_hbm,
    output, features_grad, first_grad, second_grad,
    rule_src, rule_buf, rows1_src, rows1_buf, rows2_src, rows2_buf,
    grad2_src, grad2_buf, grad1_src, grad1_buf, sum1_src, sum1_buf, sum2_src, sum2_buf,
    part2_src, part2_buf, part1_src, part1_buf, back2_src, back2_buf, back1_src, back1_buf,
    features, mask, rule, cotangent, first_stack, second_stack, loads,
    faces, edges, corners, order, order_t, raw, wide1, wide2, margin,
    ordered2, ordered1, flipped2, flipped1, running, kept_act,
    send, recv,
):
    me_s, me_c = lax.axis_index("space"), lax.axis_index("chan")
    bricks, rows = 2 * n_s, 128 * n_s
    f32, bf16 = jnp.float32, jnp.bfloat16

    def is_me(s, c):
        return jnp.logical_and(s == me_s, c == me_c)

    def remote(kind, src, buf, order, slot, s, c):
        return pltpu.make_async_remote_copy(
            src_ref=src, dst_ref=buf.at[slot], send_sem=send.at[kind, order],
            recv_sem=recv.at[kind, slot], device_id=(s, c), device_id_type=MESH,
        )

    def along(kind, src_of, buf):
        for k in range(1, n_s):
            s = lax.rem(me_s + k, n_s)
            yield remote(kind, src_of(s), buf, k, me_s, s, me_c), remote(
                kind, src_of(s), buf, k, s, s, me_c
            )

    def start_along(kind, src_of, buf):
        for out, _ in along(kind, src_of, buf):
            out.start()

    def wait_along(kind, src_of, buf):
        for _, come in along(kind, src_of, buf):
            come.wait_recv()

    def sent_along(kind, src_of, buf):
        for out, _ in along(kind, src_of, buf):
            out.wait_send()

    def if_other(s, c, act, here=None):
        pl.when(jnp.logical_not(is_me(s, c)))(act)
        if here is not None:
            pl.when(is_me(s, c))(here)

    def spread_start(kind, src, buf):
        for h in range(2):
            s, c = 2 * me_c + h, me_s % n_c

            def here():
                buf[me_s] = src[h]

            if_other(s, c, lambda: remote(kind, src.at[h], buf, h, me_s, s, c).start(), here)

    def handed_on(kind, buf, act):
        for u in range(2):
            slot = me_c + n_c * u
            for k in range(1, n_c):
                c = lax.rem(me_c + k, n_c)
                act(remote(kind, buf.at[slot], buf, 2 + u * (n_c - 1) + k - 1, slot, me_s, c))

    def spread_relay(kind, src, buf):
        for u in range(2):
            s, c = me_c + n_c * u, me_s // 2
            if_other(s, c, lambda: remote(kind, src.at[0], buf, 0, s, s, c).wait_recv())
        handed_on(kind, buf, lambda copy: copy.start())

    def spread_wait(kind, src, buf):
        for u in range(2):
            for k in range(1, n_c):
                c = lax.rem(me_c + k, n_c)
                slot = c + n_c * u
                remote(kind, src.at[0], buf, 0, slot, me_s, c).wait_recv()

    def spread_sent(kind, src, buf):
        for h in range(2):
            s, c = 2 * me_c + h, me_s % n_c
            if_other(s, c, lambda: remote(kind, src.at[h], buf, h, me_s, s, c).wait_send())
        handed_on(kind, buf, lambda copy: copy.wait_send())

    def parts(kind, src, buf, act):
        for k in range(1, n_c):
            c = lax.rem(me_c + k, n_c)
            act(remote(kind, src.at[c], buf, k, me_c, me_s, c))

    def owners(kind, src, buf, act, here=None):
        for u in range(2):
            s, c = me_c + n_c * u, me_s // 2

            def keep():
                buf[me_s % 2] = src[u]

            if_other(
                s, c, lambda: act(remote(kind, src.at[u], buf, u, me_s % 2, s, c)), keep if here else None
            )

    def parts_start(kind, src, buf):
        buf[me_c] = src[me_c]
        parts(kind, src, buf, lambda copy: copy.start())

    def parts_relay(kind, src, buf, next_kind, next_src, next_buf):
        for k in range(1, n_c):
            c = lax.rem(me_c + k, n_c)
            remote(kind, src.at[c], buf, k, c, me_s, c).wait_recv()
        total = buf[0].astype(f32)
        for c in range(1, n_c):
            total = total + buf[c].astype(f32)
        next_src[...] = total
        owners(next_kind, next_src, next_buf, lambda copy: copy.start(), True)

    def owners_wait(kind, src, buf):
        for h in range(2):
            s, c = 2 * me_c + h, me_s % n_c
            if_other(s, c, lambda: remote(kind, src.at[0], buf, 0, h, s, c).wait_recv())

    fetched = [
        pltpu.make_async_copy(src, dst, loads.at[i])
        for i, (src, dst) in enumerate(
            (
                (mask_hbm, mask), (features_hbm, features), (cotangent_hbm, cotangent), (rule_hbm, rule),
                (first_hbm, first_stack.at[:, 0:3]), (second_hbm, second_stack.at[:, 0:3]),
            )
        )
    ]
    for copy in fetched:
        copy.start()

    barrier = pltpu.get_barrier_semaphore()

    def greet(s, c):
        pl.semaphore_signal(barrier, inc=1, device_id=(s, c), device_id_type=MESH)

    for k in range(1, n_s):
        greet(lax.rem(me_s + k, n_s), me_c)
    for k in range(1, n_c):
        greet(me_s, lax.rem(me_c + k, n_c))
    for h in range(2):
        s, c = 2 * me_c + h, me_s % n_c
        if_other(s, c, lambda: greet(s, c))
        s, c = me_c + n_c * h, me_s // 2
        if_other(s, c, lambda: greet(s, c))

    for copy in fetched[:4]:
        copy.wait()

    square = (128, 128)
    diagonal = lax.broadcasted_iota(jnp.int32, square, 0) == lax.broadcasted_iota(jnp.int32, square, 1)
    active = jnp.sum(jnp.where(diagonal, mask[...].astype(f32), 0.0), axis=1, keepdims=True)
    masked = features[...].astype(f32) * active
    for h, part in enumerate(halves_packed(masked)):
        rows1_src[h] = part.astype(bf16)
    grad2 = (cotangent[...].astype(f32) * active).astype(bf16)
    grad2_src[...] = grad2
    grad2_buf[me_s] = grad2
    rule_src[...] = jnp.zeros(rule_src.shape, jnp.int32)
    rule_src[0:2, 0:27] = rule[...]
    place = lax.broadcasted_iota(jnp.int32, (bricks, 128), 0)
    own_rule = jnp.where(place == 2 * me_s, rule_src[0:1, :], 0) + jnp.where(
        place == 2 * me_s + 1, rule_src[1:2, :], 0
    )
    rule_src[...] = own_rule
    rule_buf[me_s] = own_rule

    greeted = n_s + n_c + 2 - 2 * jnp.where(is_me(2 * me_c + me_s % 2, me_s % n_c), 1, 0)
    pl.semaphore_wait(barrier, greeted)
    start_along(RULE, lambda s: rule_src, rule_buf)
    spread_start(ROWS1, rows1_src, rows1_buf)
    start_along(GRAD2, lambda s: grad2_src, grad2_buf)

    lane = lax.broadcasted_iota(jnp.int32, (16, rows), 1)
    natural = (lane % bricks) * 64 + lane // bricks
    deep = lax.broadcasted_iota(jnp.int32, (16, rows), 0)

    def order_step(r, carry):
        at = pl.multiple_of(r * 16, 16)
        order_t[pl.ds(at, 16), :] = jnp.where(deep + at == natural, 1.0, 0.0).astype(bf16)
        order[pl.ds(at, 16), :] = jnp.where(deep * 64 + r == lane, 1.0, 0.0).astype(bf16)
        return carry

    lax.fori_loop(0, rows // 16, order_step, 0)
    for stack in (first_stack, second_stack):
        stack[:, 3] = jnp.zeros((9, 64, 128), bf16)
    spread_relay(ROWS1, rows1_src, rows1_buf)

    wait_along(RULE, lambda s: rule_src, rule_buf)
    whole_rule = rule_buf[0]
    for s in range(1, n_s):
        whole_rule = whole_rule + rule_buf[s]
    whole_rule = jnp.where(whole_rule < 0, -4096, whole_rule)
    which = {16: faces, 4: edges, 1: corners}
    for c, cells, at, _, _ in brick_offsets():
        fed = jnp.broadcast_to(whole_rule[:, c : c + 1], (bricks, 128))
        span = cells * bricks
        for cell in range(cells):
            for part in range(0, span, 128):
                width = min(128, span - part)
                hit = lane[:, :128] + (part - cell * bricks) == fed
                which[cells][at, cell * bricks : (cell + 1) * bricks, part : part + width] = (
                    jnp.where(hit, 1.0, 0.0).astype(bf16)[:, :width]
                )

    slab = EDGE * EDGE * bricks

    def widen(buf, wide):
        parts = []
        for s in range(n_s):
            block = buf[s].astype(f32)
            back = turned(block)
            low = low_lanes(block.shape)
            parts.append(jnp.where(low, block, back))
            parts.append(jnp.where(low, back, block))
        doubled = jnp.concatenate(parts, 0).astype(bf16)

        for i in range(4):
            got = jnp.dot(order[i * 256 : (i + 1) * 256, :], doubled, preferred_element_type=f32)
            raw[i + 1, 1:5, 1:5] = got.reshape(4, 4, bricks, 128).astype(bf16)
        for c, cells, at, target, source in brick_offsets():
            value = raw[source].reshape(cells * bricks, 128)
            got = jnp.dot(which[cells][at], value, preferred_element_type=f32)
            raw[target] = got.astype(bf16).reshape(raw[target].shape)

        def step(i, carry):
            got = raw[i].astype(f32)
            after = jnp.concatenate([got[:, 1:], got[:, EDGE - 1 :]], 1)
            wide[i] = jnp.where(low_lanes(got.shape), got, after).astype(bf16)
            return carry

        lax.fori_loop(0, EDGE, step, 0)

    def taps(wide, i, depth_i, dy):
        chunk = depth_i * 16 * bricks
        near = wide[pl.ds(i, depth_i), pl.ds(dy, 4), 0:4].reshape(chunk, 128)
        far = wide[pl.ds(i, depth_i), pl.ds(dy, 4), 2:6].reshape(chunk, 128)
        return jnp.concatenate([near, far], 1)

    def convolve(wide, weight, target, buf):
        chunk = 16 * bricks

        def step(i, carry):
            total = jnp.zeros((chunk, 128), f32)
            for q in range(9):
                total = total + jnp.dot(
                    taps(wide, i + q // 3, 1, q % 3), weight[q].reshape(256, 128), preferred_element_type=f32
                )
            running[pl.ds(pl.multiple_of(i * chunk, chunk), chunk), :] = total.astype(bf16)
            return carry

        lax.fori_loop(0, 4, step, 0)
        whole = jnp.dot(order_t[...], running[...], preferred_element_type=f32)
        target[...] = whole.astype(bf16).reshape(n_s, 128, 128)
        buf[me_s] = target[me_s]

    def reorder(buf, ordered, flipped):
        whole = buf[...].reshape(rows, 128)
        for i in range(4):
            got = jnp.dot(order[i * 256 : (i + 1) * 256, :], whole, preferred_element_type=f32)
            ordered[i * 256 : (i + 1) * 256, :] = got.astype(bf16)
            flipped[:, i * 256 : (i + 1) * 256] = got.T.astype(bf16)

    def transposed(ordered, weight, target):
        margin[...] = jnp.zeros(margin.shape, f32)
        chunk = 16 * bricks

        def step(q, carry):
            dx, dy = q // 3, q % 3
            kernel = weight[q].reshape(256, 128)
            for i in range(4):
                part = lax.dot_general(
                    ordered[i * chunk : (i + 1) * chunk, :], kernel,
                    (((1,), (1,)), ((), ())), preferred_element_type=f32,
                )
                near = part[:, :128].reshape(1, 4, 4, bricks, 128)
                far = part[:, 128:].reshape(1, 4, 4, bricks, 128)
                margin[pl.ds(i + dx, 1), pl.ds(dy, 4), 0:4] += near
                margin[pl.ds(i + dx, 1), pl.ds(dy, 4), 2:6] += far
            return carry

        lax.fori_loop(0, 9, step, 0)

        def fold(i, carry):
            value = margin[i]
            before = jnp.concatenate([jnp.zeros_like(value[:, :1]), value[:, : EDGE - 1]], 1)
            both = jnp.where(low_lanes(value.shape), value, before).reshape(slab, 128)
            margin[i] = (both + turned(both)).reshape(value.shape)
            return carry

        lax.fori_loop(0, EDGE, fold, 0)
        for c, cells, at, source, owner in brick_offsets():
            value = margin[source].reshape(cells * bricks, 128)
            coarse = value.astype(bf16).astype(f32)
            split = jnp.where(low_lanes(value.shape), coarse, value - coarse).astype(bf16)
            got = lax.dot_general(
                which[cells][at], split, (((0,), (0,)), ((), ())), preferred_element_type=f32
            )
            margin[owner] += (got + turned(got)).reshape(margin[owner].shape)
        running[...] = margin[1:5, 1:5, 1:5].reshape(rows, 128).astype(bf16)

        got = jnp.dot(order_t[...], running[...], preferred_element_type=f32)
        for s in range(n_s):
            upper, lower = got[s * 128 : s * 128 + 64], got[s * 128 + 64 : s * 128 + 128]
            target[s % n_c, s // n_c] = jnp.where(low_lanes(upper.shape), upper, lower).astype(bf16)

    def kernel_grad(wide, flipped, target):
        def step(q, carry):
            got = jnp.dot(flipped[...], taps(wide, q // 3, 4, q % 3), preferred_element_type=f32)
            target[pl.ds(3 * q, 3)] = got.T[:192].reshape(3, 64, 128)
            return carry

        lax.fori_loop(0, 9, step, 0)

    def summed(buf):
        total = buf[0].astype(f32)
        for s in range(1, n_s):
            total = total + buf[s].astype(f32)
        return total

    def returned(buf):
        sums = (buf[0], buf[1])
        low = low_lanes(sums[0].shape)
        return jnp.concatenate(
            [
                jnp.where(low, sums[0], turned(sums[1])),
                jnp.where(low, turned(sums[0]), sums[1]),
            ],
            0,
        )

    for copy in fetched[4:]:
        copy.wait()
    spread_wait(ROWS1, rows1_src, rows1_buf)
    widen(rows1_buf, wide1)
    convolve(wide1, first_stack, sum1_src, sum1_buf)
    start_along(SUM1, lambda s: sum1_src.at[s], sum1_buf)
    wait_along(GRAD2, lambda s: grad2_src, grad2_buf)
    reorder(grad2_buf, ordered2, flipped2)
    transposed(ordered2, second_stack, part2_src)
    parts_start(PART2, part2_src, part2_buf)

    wait_along(SUM1, lambda s: sum1_src.at[s], sum1_buf)
    act = active * summed(sum1_buf)
    hidden = act * jax.nn.sigmoid(act)
    for h, part in enumerate(halves_packed(hidden)):
        rows2_src[h] = part.astype(bf16)
    spread_start(ROWS2, rows2_src, rows2_buf)
    kept_act[...] = act
    parts_relay(PART2, part2_src, part2_buf, BACK2, back2_src, back2_buf)
    spread_relay(ROWS2, rows2_src, rows2_buf)

    owners_wait(BACK2, back2_src, back2_buf)
    act = kept_act[...]
    gate = jax.nn.sigmoid(act)
    grad1 = (active * returned(back2_buf) * gate * (1.0 + act * (1.0 - gate))).astype(bf16)
    grad1_src[...] = grad1
    grad1_buf[me_s] = grad1
    start_along(GRAD1, lambda s: grad1_src, grad1_buf)

    spread_wait(ROWS2, rows2_src, rows2_buf)
    widen(rows2_buf, wide2)
    convolve(wide2, second_stack, sum2_src, sum2_buf)
    start_along(SUM2, lambda s: sum2_src.at[s], sum2_buf)
    wait_along(GRAD1, lambda s: grad1_src, grad1_buf)
    reorder(grad1_buf, ordered1, flipped1)
    transposed(ordered1, first_stack, part1_src)
    parts_start(PART1, part1_src, part1_buf)

    kernel_grad(wide2, flipped2, second_grad)
    parts_relay(PART1, part1_src, part1_buf, BACK1, back1_src, back1_buf)
    kernel_grad(wide1, flipped1, first_grad)

    wait_along(SUM2, lambda s: sum2_src.at[s], sum2_buf)
    output[...] = (active * summed(sum2_buf)).astype(bf16)
    owners_wait(BACK1, back1_src, back1_buf)
    features_grad[...] = (active * returned(back1_buf)).astype(bf16)

    sent_along(RULE, lambda s: rule_src, rule_buf)
    sent_along(GRAD2, lambda s: grad2_src, grad2_buf)
    sent_along(GRAD1, lambda s: grad1_src, grad1_buf)
    sent_along(SUM1, lambda s: sum1_src.at[s], sum1_buf)
    sent_along(SUM2, lambda s: sum2_src.at[s], sum2_buf)
    spread_sent(ROWS1, rows1_src, rows1_buf)
    spread_sent(ROWS2, rows2_src, rows2_buf)
    parts(PART2, part2_src, part2_buf, lambda copy: copy.wait_send())
    parts(PART1, part1_src, part1_buf, lambda copy: copy.wait_send())
    owners(BACK2, back2_src, back2_buf, lambda copy: copy.wait_send())
    owners(BACK1, back1_src, back1_buf, lambda copy: copy.wait_send())


def still_weights(n_s, n_c, features, mask, rulebook, weight_first, weight_second, cotangent):
    bricks, rows = 2 * n_s, 128 * n_s
    f32, bf16 = jnp.float32, jnp.bfloat16

    def stacked(weight):
        return jnp.transpose(weight, (1, 0, 2)).reshape(9, 3, 64, 128)

    def buffers(shape, kind, sources=None):
        return [pltpu.VMEM(sources or shape, kind), pltpu.VMEM(shape, kind)]

    wide = (EDGE, EDGE, EDGE, bricks, 128)
    packed, square = (n_s, 64, 128), (n_s, 128, 128)
    scratch = (
        buffers((n_s, bricks, 128), jnp.int32, (bricks, 128))
        + buffers(packed, bf16, (2, 64, 128)) * 2
        + buffers(square, bf16, (128, 128)) * 2
        + buffers(square, bf16) * 2
        + buffers((n_c, 2, 64, 128), bf16) * 2
        + buffers((2, 64, 128), f32) * 2
        + [
            pltpu.VMEM((128, 128), bf16),
            pltpu.VMEM((1, 128), jnp.int32),
            pltpu.VMEM((2, 27), jnp.int32),
            pltpu.VMEM((128, 128), bf16),
            pltpu.VMEM((9, 4, 64, 128), bf16),
            pltpu.VMEM((9, 4, 64, 128), bf16),
            pltpu.SemaphoreType.DMA((6,)),
        ]
        + [
            pltpu.VMEM((6, 256, 256), bf16),
            pltpu.VMEM((12, 64, 64), bf16),
            pltpu.VMEM((8, 16, 16), bf16),
            pltpu.VMEM((rows, rows), bf16),
            pltpu.VMEM((rows, rows), bf16),
            pltpu.VMEM(wide, bf16),
            pltpu.VMEM(wide, bf16),
            pltpu.VMEM(wide, bf16),
            pltpu.VMEM(wide, f32),
            pltpu.VMEM((rows, 128), bf16),
            pltpu.VMEM((rows, 128), bf16),
            pltpu.VMEM((128, rows), bf16),
            pltpu.VMEM((128, rows), bf16),
            pltpu.VMEM((rows, 128), bf16),
            pltpu.VMEM((128, 128), f32),
            pltpu.SemaphoreType.DMA((11, max(n_s, 2 * n_c))),
            pltpu.SemaphoreType.DMA((11, max(n_s, 2 * n_c))),
        ]
    )
    output, features_grad, first_grad, second_grad = pl.pallas_call(
        functools.partial(still_kernel, n_s, n_c),
        out_shape=[jax.ShapeDtypeStruct((128, 128), bf16)] * 2
        + [jax.ShapeDtypeStruct((27, 64, 128), f32)] * 2,
        in_specs=[pl.BlockSpec(memory_space=pltpu.HBM)] * 6,
        out_specs=[pl.BlockSpec(memory_space=pltpu.VMEM)] * 4,
        scratch_shapes=scratch,
        compiler_params=pltpu.CompilerParams(
            collective_id=0, has_side_effects=True, vmem_limit_bytes=61 * 2**20
        ),
    )(
        features, mask.reshape(1, 128), rulebook,
        stacked(weight_first), stacked(weight_second), cotangent,
    )

    def unstacked(grad):
        return jnp.transpose(grad, (1, 0, 2))

    return (
        output, features_grad, unstacked(first_grad), unstacked(second_grad),
    )


def solution(mesh):
    n_space, n_chan = mesh.shape["space"], mesh.shape["chan"]
    body = on_device
    if n_space == 8 and n_chan == 4:
        body = functools.partial(still_weights, n_space, n_chan)
    placed = (
        P("space", "chan"),
        P("space"),
        P("space", None),
        P("space", None, "chan"),
        P("space", None, "chan"),
        P("space", "chan"),
    )
    return jax.shard_map(
        body,
        mesh=mesh,
        in_specs=placed,
        out_specs=(
            P("space", "chan"),
            P("space", "chan"),
            P("space", None, "chan"),
            P("space", None, "chan"),
        ),
        check_vma=False,
    )
```
